32 devices in a mesh: space: 8 (over z, y), tm: 4 (over x, core).
Axes of the slice: x: 2, y: 2, z: 4, core: 2. Of those that a mesh axis runs over, the one named last changes fastest.
Arguments:
- pw_field: float32 [96, 128, 36864], P('space', 'tm'), may hold values from -6 to 6
- cell_area: float32 [16, 36864], replicated, may hold values from 0.5 to 1.5
- tile_ids: int32 [96], replicated, may hold values from 0 to 95, as said below
- edge_table: int32 [3, 96, 4], replicated, may hold values from 0 to 95, as said below
Outputs:
- gram: float32 [128, 128], P('tm')
The draws below stay inside these ranges and needn't reach their ends.
Inputs may be any that keep to these rules, and one draw needn't show every extreme that they name: A permutation: slot s holds the tile of face tile_ids[s] // 16, row (tile_ids[s] // 4) mod 4, column tile_ids[s] mod 4 of the face. `edge_table`: the cube's gluing for the slots of tile_ids: the neighbour slot and edge across each edge, and 1 where the two edges run in opposite directions; flags and edges lie in 0 to 1 and 0 to 3.
All inputs are finite; a program needn't handle non-finite values.
Results may differ from the reference program's by a relative error of at most 0.000051.
Values sent between devices are 32-bit elements; how exact they have to be, the bound alone decides.
A program may use at most 704 MiB of HBM per device.

```python
import math
import jax
import jax.numpy as jnp
from jax import lax

SUB = 4
STRIDE = 4
STEPS = 4
TILE = 192
TILES = 96
SNAPS = 128


FRAMES = [((1, 0, 0), (0, 1, 0), (0, 0, 1)), ((0, 1, 0), (-1, 0, 0), (0, 0, 1)), ((-1, 0, 0), (0, -1, 0), (0, 0, 1)), ((0, -1, 0), (1, 0, 0), (0, 0, 1)), ((0, 0, 1), (0, 1, 0), (-1, 0, 0)), ((0, 0, -1), (0, 1, 0), (1, 0, 0))]


def corner_key(center, axis_u, axis_v, coord_a, coord_b, sub_count):
    return tuple((sub_count * center[index_c] + coord_a * axis_u[index_c] + coord_b * axis_v[index_c] for index_c in range(3)))


def cube_table(sub_count):
    tiles_total = 6 * sub_count * sub_count
    records = {}
    for face_idx in range(6):
        center, axis_u, axis_v = FRAMES[face_idx]
        for row_tile in range(sub_count):
            for col_tile in range(sub_count):
                tile_idx = face_idx * sub_count * sub_count + row_tile * sub_count + col_tile
                low_a = -sub_count + 2 * row_tile
                high_a = low_a + 2
                low_b = -sub_count + 2 * col_tile
                high_b = low_b + 2
                edge_ends = [((low_a, low_b), (low_a, high_b)), ((high_a, low_b), (high_a, high_b)), ((low_a, low_b), (high_a, low_b)), ((low_a, high_b), (high_a, high_b))]
                for edge_idx in range(4):
                    end_keys = []
                    for coord_a, coord_b in edge_ends[edge_idx]:
                        end_keys.append(corner_key(center, axis_u, axis_v, coord_a, coord_b, sub_count))
                    joint_key = tuple(sorted(end_keys))
                    entry = (tile_idx, edge_idx, end_keys[0])
                    if joint_key in records:
                        records[joint_key].append(entry)
                    else:
                        records[joint_key] = [entry]
    near_tile = [[0] * 4 for _ in range(tiles_total)]
    near_edge = [[0] * 4 for _ in range(tiles_total)]
    near_flip = [[0] * 4 for _ in range(tiles_total)]
    for paired in records.values():
        for own_end, far_end in ((paired[0], paired[1]), (paired[1], paired[0])):
            near_tile[own_end[0]][own_end[1]] = far_end[0]
            near_edge[own_end[0]][own_end[1]] = far_end[1]
            near_flip[own_end[0]][own_end[1]] = 0 if own_end[2] == far_end[2] else 1
    return (near_tile, near_edge, near_flip)


def slot_layout(key):
    order = jax.random.permutation(key, TILES).astype(jnp.int32)
    near_tile, near_edge, near_flip = cube_table(SUB)
    tile_table = jnp.asarray(near_tile, dtype=jnp.int32)
    edge_list = jnp.asarray(near_edge, dtype=jnp.int32)
    flip_list = jnp.asarray(near_flip, dtype=jnp.int32)
    slot_of = jnp.zeros((TILES,), jnp.int32).at[order].set(jnp.arange(TILES, dtype=jnp.int32))
    near_slot = slot_of[tile_table[order]]
    table = jnp.stack([near_slot, edge_list[order], flip_list[order]])
    return (order, table.astype(jnp.int32))


def draw_tile_ids(key, part):
    layout = slot_layout(key)
    key = jax.random.fold_in(key, 1)
    return layout[0]


def draw_edge_table(key, part):
    layout = slot_layout(key)
    key = jax.random.fold_in(key, 2)
    return layout[1]


def draw_pw_field(key, part):
    key = jax.random.fold_in(key, 3)
    sub_keys = jax.random.split(key, 4)
    full_shape = (TILES, SNAPS, TILE * TILE)
    rough_part = jax.random.normal(sub_keys[0], full_shape, jnp.float32)
    return jnp.clip(rough_part, -6.0, 6.0)


def setup_inputs(seed: int = 0) -> dict:
    key_list = jax.random.split(jax.random.key(seed), 5)
    pw_field = draw_pw_field(jax.random.fold_in(key_list[4], 71), 0)
    cell_area = jnp.clip(jnp.exp(jax.random.uniform(key_list[1], (SUB * SUB, TILE * TILE), jnp.float32, math.log(0.5), math.log(1.5))), 0.5, 1.5)
    tile_ids = draw_tile_ids(jax.random.fold_in(key_list[4], 71), 0)
    edge_table = draw_edge_table(jax.random.fold_in(key_list[4], 71), 0)
    return {"pw_field": pw_field, "cell_area": cell_area, "tile_ids": tile_ids, "edge_table": edge_table}


def coefficient(step_idx):
    return 0.12 + 0.1 * step_idx / max(STEPS - 1, 1)


def edge_strips(weighted):
    return jnp.stack([weighted[:, :, :TILE], weighted[:, :, -TILE:], weighted[:, :, 0::TILE], weighted[:, :, TILE - 1::TILE]], axis=1)


def pick_halo(all_strips, near_slot, near_edge, near_flip):
    snap_count = all_strips.shape[2]
    edge_width = all_strips.shape[3]
    flat_strips = all_strips.reshape(-1, snap_count, edge_width)
    position = (near_slot * 4 + near_edge).reshape(-1)
    chosen = jnp.take(flat_strips, position, axis=0).reshape(near_slot.shape[0], 4, snap_count, edge_width)
    return jnp.where((near_flip == 1)[:, :, None, None], chosen[..., ::-1], chosen)


def smooth_step(values, weighted, tile_area, halo_rows, factor):
    column = jnp.arange(TILE * TILE, dtype=jnp.int32) % TILE
    upper_nb = jnp.concatenate([halo_rows[:, 0], weighted[:, :, :-TILE]], axis=2)
    lower_nb = jnp.concatenate([weighted[:, :, TILE:], halo_rows[:, 1]], axis=2)
    left_shift = jnp.concatenate([weighted[:, :, :1], weighted[:, :, :-1]], axis=2)
    right_shift = jnp.concatenate([weighted[:, :, 1:], weighted[:, :, -1:]], axis=2)
    left_nb = jnp.where(column == 0, jnp.repeat(halo_rows[:, 2], TILE, axis=2), left_shift)
    right_nb = jnp.where(column == TILE - 1, jnp.repeat(halo_rows[:, 3], TILE, axis=2), right_shift)
    return values + factor * (upper_nb + lower_nb + left_nb + right_nb - 4.0 * weighted) / tile_area[:, None]


def subsample(values):
    shaped = values.reshape(values.shape[0], values.shape[1], TILE, TILE)[:, :, 1::STRIDE, 1::STRIDE]
    return shaped.reshape(values.shape[0], values.shape[1], -1)


def reference(pw_field, cell_area, tile_ids, edge_table):
    tile_area = jnp.take(cell_area, tile_ids % cell_area.shape[0], axis=0)

    def one_snapshot(snap_index):
        values = lax.dynamic_slice_in_dim(pw_field, snap_index, 1, 1)
        for step_idx in range(STEPS):
            weighted = tile_area[:, None] * values
            halo_rows = pick_halo(edge_strips(weighted), edge_table[0], edge_table[1], edge_table[2])
            values = smooth_step(values, weighted, tile_area, halo_rows, coefficient(step_idx))
        return subsample(values)[:, 0]

    sampled = lax.map(one_snapshot, jnp.arange(SNAPS, dtype=jnp.int32))
    snap_rows = sampled.reshape(SNAPS, -1)
    weights = subsample(tile_area[:, None])[:, 0].reshape(-1)
    full_gram = jnp.dot(snap_rows * weights, snap_rows.T, precision=lax.Precision.HIGHEST, preferred_element_type=jnp.float32)
    return full_gram / snap_rows.shape[1]
```

```python
import functools
import jax
import jax.numpy as jnp
import ml_dtypes
import numpy as np
from jax import lax
from jax.experimental import pallas as pl
from jax.experimental.pallas import tpu as pltpu
from jax.sharding import PartitionSpec as P

STRIDE = 4
STEPS = 4
TILE = 192
SIDE = TILE // STRIDE
ROWS = 2 * STRIDE
CHUNKS = TILE // ROWS
DEPTH = ROWS * TILE
RIM = 4 * TILE
LANES = 128
HALF = 64
F32, BF16 = jnp.float32, jnp.bfloat16
VMEM_LIMIT = 56 * 1024 * 1024


def coefficient(step_idx):
    return 0.12 + 0.1 * step_idx / max(STEPS - 1, 1)


def stencil_taps():
    taps = np.zeros((2 * STEPS + 1, 2 * STEPS + 1))
    taps[STEPS, STEPS] = 1.0
    for step_idx in range(STEPS):
        padded = np.pad(taps, 1)
        lap = (
            padded[:-2, 1:-1] + padded[2:, 1:-1] + padded[1:-1, :-2] + padded[1:-1, 2:] - 4 * taps
        )
        taps = taps + coefficient(step_idx) * lap
    return taps


TAPS = stencil_taps()
CORNER = 3.0 * float(np.prod([coefficient(k) for k in range(STEPS)]))


def response(row, col, first_row, row_count):
    plane = np.zeros((row_count, TILE))
    for d_row in range(-STEPS, STEPS + 1):
        for d_col in range(-STEPS, STEPS + 1):
            at_row, at_col = row + d_row - first_row, col + d_col
            if 0 <= at_row < row_count and 0 <= at_col < TILE:
                plane[at_row, at_col] = TAPS[d_row + STEPS, d_col + STEPS]
    return plane.reshape(-1)


def split_const(matrix):
    high = matrix.astype(ml_dtypes.bfloat16)
    low = (matrix - high.astype(np.float64)).astype(ml_dtypes.bfloat16)
    return high, low


def along(variant, index):
    return TILE - 2 - STRIDE * index if variant % 2 else 1 + STRIDE * index


def beyond(variant):
    return 3 if variant // 2 else 2


def chunk_matrix():
    matrix = np.zeros((DEPTH, 2 * LANES))

    def put(lane, slot, row, col):
        matrix[:, lane] = response(row, col, 0, ROWS)
        other = row + ROWS if slot == 0 else row - ROWS
        matrix[:, LANES + lane] = response(other, col, 0, ROWS)

    for slot in range(2):
        for index in range(SIDE):
            put(slot * SIDE + index, slot, 1 + STRIDE * slot, 1 + STRIDE * index)
        for side in range(2):
            for variant in range(4):
                col = TILE - 1 + beyond(variant) if side else -beyond(variant)
                row = (2 if variant % 2 else 1) + STRIDE * slot
                put(2 * SIDE + side * 8 + variant * 2 + slot, slot, row, col)
    return matrix


def rim_matrices():
    upper = np.zeros((RIM, 4 * LANES))
    lower = np.zeros((RIM, 4 * LANES))
    for variant in range(4):
        base = variant * LANES
        for index in range(SIDE):
            col = along(variant, index)
            upper[:, base + index] = response(-beyond(variant), col, 0, 4)
            lower[:, base + HALF + index] = response(
                TILE - 1 + beyond(variant), col, TILE - 4, 4
            )
        upper[0, base + SIDE] = 1.0
        upper[TILE - 1, base + SIDE + 1] = 1.0
        lower[3 * TILE, base + HALF + SIDE] = 1.0
        lower[4 * TILE - 1, base + HALF + SIDE + 1] = 1.0
    return upper, lower


def order_matrix():
    matrix = np.zeros((CHUNKS * 16, 4 * LANES))
    for chunk in range(CHUNKS):
        for side in range(2):
            for variant in range(4):
                for slot in range(2):
                    index = 2 * chunk + slot
                    place = SIDE - 1 - index if variant % 2 else index
                    source = chunk * 16 + side * 8 + variant * 2 + slot
                    matrix[source, variant * LANES + side * HALF + place] = 1.0
    return matrix.astype(ml_dtypes.bfloat16)


def place_matrix():
    matrix = np.zeros((CHUNKS, 2 * LANES, LANES))
    for index in range(SIDE):
        chunk, slot = index // 2, index % 2
        matrix[0, index, index] = 1.0
        matrix[CHUNKS - 1, HALF + index, SIDE + index] = 1.0
        matrix[chunk, LANES + index, slot * SIDE] = 1.0
        matrix[chunk, LANES + HALF + index, slot * SIDE + SIDE - 1] = 1.0
    for lane in (SIDE, SIDE + 1, HALF + SIDE, HALF + SIDE + 1):
        matrix[0, lane, 0] = 1.0
    return matrix.astype(ml_dtypes.bfloat16)


def split(x):
    high = x.astype(BF16)
    return high, (x - high.astype(F32)).astype(BF16)


def dot(a, b):
    return jnp.dot(a, b, preferred_element_type=F32)


def dot3(a_high, a_low, b_high, b_low):
    return dot(a_high, b_high) + dot(a_low, b_high) + dot(a_high, b_low)


def stencil_kernel(
    tiles, snaps, slots, faces,
    first_ref, ids_ref, table_ref,
    x_ref, area_ref, main_h, main_l, up_h, up_l, down_h, down_l, order_ref,
    out_ref, send_ref,
    high, low, carry, edges, rims,
):
    step = pl.program_id(0)
    first = first_ref[0]
    rows = tiles * snaps
    for t in range(tiles):
        face = lax.rem(ids_ref[first + t], faces)
        part = pl.ds(t * snaps, snaps)
        h, l = split(x_ref[t] * area_ref[pl.ds(face, 1), :])
        high[part, :] = h
        low[part, :] = l
    lane = lax.broadcasted_iota(jnp.int32, (rows, LANES), 1)
    from_before = (lane < SIDE) | ((lane >= 2 * SIDE) & (lane % 2 == 0))
    is_edge = (lane >= 2 * SIDE) & (lane < 2 * SIDE + 16)

    def collect(chunk, value):
        shift = lax.rem(16 * lax.rem(chunk, 8) + LANES - 2 * SIDE, LANES)
        block = lax.div(chunk, 8)
        edges[block] = edges[block] + pltpu.roll(jnp.where(is_edge, value, 0.0), shift, 1)

    @pl.when(step == 0)
    def _():
        carry[...] = jnp.zeros_like(carry)
        edges[...] = jnp.zeros_like(edges)
        rims[...] = dot3(high[:, :RIM], low[:, :RIM], up_h[...], up_l[...])

    result = dot3(high[...], low[...], main_h[...], main_l[...])
    own, other = result[:, :LANES], result[:, LANES:]

    @pl.when(step > 0)
    def _():
        done = out_ref[step - 1] + jnp.where(from_before, 0.0, other)
        out_ref[step - 1] = done
        collect(step - 1, done)

    own = own + jnp.where(from_before, carry[...], 0.0)
    out_ref[step] = own
    carry[...] = other

    @pl.when(step == CHUNKS - 1)
    def _():
        collect(step, own)
        rims[...] = rims[...] + dot3(
            high[:, DEPTH - RIM :], low[:, DEPTH - RIM :], down_h[...], down_l[...]
        )
        sides = jnp.zeros((rows, 4 * LANES), F32)
        for block in range(CHUNKS * 16 // LANES):
            h, l = split(edges[block])
            matrix = order_ref[block * LANES : (block + 1) * LANES, :]
            sides = sides + dot(h, matrix) + dot(l, matrix)
        low_half = lane[:snaps] < HALF
        for t in range(tiles):
            part = slice(t * snaps, (t + 1) * snaps)
            for pair, source in ((0, rims[part, :]), (1, sides[part, :])):
                chosen = jnp.zeros((snaps, LANES), F32)
                at = (first + t) * 4 + 2 * pair
                kind = [
                    2 * lax.rem(table_ref[slots * 4 + at + k], 2) + table_ref[slots * 8 + at + k]
                    for k in range(2)
                ]
                for variant in range(4):
                    block = source[:, variant * LANES : (variant + 1) * LANES]
                    wanted = jnp.where(
                        low_half,
                        (kind[0] == variant).astype(jnp.int32),
                        (kind[1] == variant).astype(jnp.int32),
                    )
                    chosen = jnp.where(wanted == 1, block, chosen)
                send_ref[t, pair] = chosen


def halo_kernel(
    tiles, snaps, slots, faces, per_step,
    first_ref, ids_ref, table_ref,
    strips_ref, sums_ref, root_ref, place_ref,
    out_ref,
    high, low,
):
    step = pl.program_id(0)
    first = first_ref[0]
    lane = lax.broadcasted_iota(jnp.int32, (snaps, LANES), 1)

    def near(slot, edge):
        at = slot * 4 + edge
        return table_ref[at], table_ref[slots * 4 + at], table_ref[slots * 8 + at]

    def corner(slot, edge):
        mid, mid_edge, mid_flip = near(slot, edge)
        other_edge = jnp.where(mid_edge < 2, 2, 0) + mid_flip
        end = lax.rem(mid_edge, 2)
        far, far_edge, far_flip = near(mid, other_edge)
        far_end = jnp.where(far_flip == 1, 1 - end, end)
        side = lax.rem(far_edge, 2)
        row_end = jnp.where(far_edge < 2, side, far_end)
        col_end = jnp.where(far_edge < 2, far_end, side)
        value = strips_ref[far, 0]
        return jnp.where(lane == SIDE + col_end + HALF * row_end, value, 0.0)

    @pl.when(step == 0)
    def _():
        for t in range(tiles):
            slot = first + t
            part = pl.ds(t * snaps, snaps)
            for pair in range(2):
                strips = []
                for k in range(2):
                    far, far_edge, _ = near(slot, 2 * pair + k)
                    value = strips_ref[far, lax.div(far_edge, 2)]
                    rolled = pltpu.roll(value, HALF, 1)
                    same = (jnp.zeros((snaps, LANES), jnp.int32) + lax.rem(far_edge, 2)) == k
                    strips.append(jnp.where(same, value, rolled))
                both = jnp.where(lane < HALF, strips[0], strips[1])
                both = jnp.where(lane % HALF < SIDE, both, 0.0)
                if pair == 0:
                    both = both + CORNER * (corner(slot, 0) + corner(slot, 2))
                h, l = split(both)
                high[part, pair * LANES : (pair + 1) * LANES] = h
                low[part, pair * LANES : (pair + 1) * LANES] = l

    for chunk in range(per_step):
        added = dot(high[...], place_ref[chunk]) + dot(low[...], place_ref[chunk])
        for t in range(tiles):
            part = slice(t * snaps, (t + 1) * snaps)
            face = lax.rem(ids_ref[first + t], faces)
            out_ref[chunk, part, :] = (sums_ref[chunk, part, :] + added[part, :]) * root_ref[
                chunk, pl.ds(face, 1), :
            ]


def gram_kernel(tiles, snaps, groups, scale, x_ref, out_ref, main, cross):
    step = pl.program_id(0)

    @pl.when(step == 0)
    def _():
        main[...] = jnp.zeros_like(main)
        cross[...] = jnp.zeros_like(cross)

    dims = (((1,), (1,)), ((), ()))
    count = groups * snaps
    highs, lows = [], []
    for t in range(tiles):
        x = x_ref[:, 0, t * snaps : (t + 1) * snaps, :].reshape(count, LANES)
        h, l = split(x)
        highs.append(h)
        lows.append(l)
    h = jnp.concatenate(highs, axis=1)
    l = jnp.concatenate(lows, axis=1)
    main[...] += lax.dot_general(h, h, dims, preferred_element_type=F32)
    cross[...] += lax.dot_general(h, l, dims, preferred_element_type=F32)

    @pl.when(step == pl.num_programs(0) - 1)
    def _():
        out_ref[...] = (main[...] + cross[...] + cross[...].T) * scale


def full(shape):
    return pl.BlockSpec(shape, lambda c, *_: (0,) * len(shape))


def body(groups, pw_field, cell_area, tile_ids, edge_table):
    tiles, snaps, cells = pw_field.shape
    slots, faces = tile_ids.shape[0], cell_area.shape[0]
    rows = tiles * snaps
    first = (lax.axis_index("space") * tiles).astype(jnp.int32).reshape(1)
    table = edge_table.reshape(-1)
    main_h, main_l = split_const(chunk_matrix())
    upper, lower = rim_matrices()
    up_h, up_l = split_const(upper)
    down_h, down_l = split_const(lower)

    sums, send = pl.pallas_call(
        functools.partial(stencil_kernel, tiles, snaps, slots, faces),
        grid_spec=pltpu.PrefetchScalarGridSpec(
            num_scalar_prefetch=3,
            grid=(CHUNKS,),
            in_specs=[
                pl.BlockSpec((tiles, snaps, DEPTH), lambda c, *_: (0, 0, c)),
                pl.BlockSpec((faces, DEPTH), lambda c, *_: (0, c)),
                full((DEPTH, 2 * LANES)),
                full((DEPTH, 2 * LANES)),
                full((RIM, 4 * LANES)),
                full((RIM, 4 * LANES)),
                full((RIM, 4 * LANES)),
                full((RIM, 4 * LANES)),
                full((CHUNKS * 16, 4 * LANES)),
            ],
            out_specs=[full((CHUNKS, rows, LANES)), full((tiles, 2, snaps, LANES))],
            scratch_shapes=[
                pltpu.VMEM((rows, DEPTH), BF16),
                pltpu.VMEM((rows, DEPTH), BF16),
                pltpu.VMEM((rows, LANES), F32),
                pltpu.VMEM((CHUNKS * 16 // LANES, rows, LANES), F32),
                pltpu.VMEM((rows, 4 * LANES), F32),
            ],
        ),
        out_shape=[
            jax.ShapeDtypeStruct((CHUNKS, rows, LANES), F32),
            jax.ShapeDtypeStruct((tiles, 2, snaps, LANES), F32),
        ],
        compiler_params=pltpu.CompilerParams(vmem_limit_bytes=VMEM_LIMIT),
        name="stencil",
    )(
        first, tile_ids, table, pw_field, cell_area,
        main_h, main_l, up_h, up_l, down_h, down_l, order_matrix(),
    )

    strips = lax.all_gather(send, "space", axis=0, tiled=True)

    sampled = cell_area.reshape(faces, TILE, TILE)[:, 1::STRIDE, 1::STRIDE]
    root = jnp.sqrt(1.0 / sampled).reshape(faces, CHUNKS, 2 * SIDE)
    root = jnp.pad(root, ((0, 0), (0, 0), (0, LANES - 2 * SIDE)))
    root = jnp.transpose(root, (1, 0, 2))

    per_step = CHUNKS // groups
    scaled = pl.pallas_call(
        functools.partial(halo_kernel, tiles, snaps, slots, faces, per_step),
        grid_spec=pltpu.PrefetchScalarGridSpec(
            num_scalar_prefetch=3,
            grid=(groups,),
            in_specs=[
                full((slots, 2, snaps, LANES)),
                pl.BlockSpec((per_step, rows, LANES), lambda c, *_: (c, 0, 0)),
                pl.BlockSpec((per_step, faces, LANES), lambda c, *_: (c, 0, 0)),
                pl.BlockSpec((per_step, 2 * LANES, LANES), lambda c, *_: (c, 0, 0)),
            ],
            out_specs=pl.BlockSpec((per_step, rows, LANES), lambda c, *_: (c, 0, 0)),
            scratch_shapes=[
                pltpu.VMEM((rows, 2 * LANES), BF16),
                pltpu.VMEM((rows, 2 * LANES), BF16),
            ],
        ),
        out_shape=jax.ShapeDtypeStruct((CHUNKS, rows, LANES), F32),
        compiler_params=pltpu.CompilerParams(vmem_limit_bytes=VMEM_LIMIT),
        name="halo",
    )(first, tile_ids, table, strips, sums, root, place_matrix())

    shared = lax.all_to_all(
        scaled.reshape(groups, per_step, rows, LANES), "tm", split_axis=0, concat_axis=0
    )
    count = groups * snaps
    partial_gram = pl.pallas_call(
        functools.partial(gram_kernel, tiles, snaps, groups, 1.0 / (slots * SIDE * SIDE)),
        grid=(per_step,),
        in_specs=[pl.BlockSpec((groups, 1, rows, LANES), lambda c: (0, c, 0, 0))],
        out_specs=pl.BlockSpec((count, count), lambda c: (0, 0)),
        scratch_shapes=[pltpu.VMEM((count, count), F32), pltpu.VMEM((count, count), F32)],
        out_shape=jax.ShapeDtypeStruct((count, count), F32),
        compiler_params=pltpu.CompilerParams(vmem_limit_bytes=VMEM_LIMIT),
        name="gram",
    )(shared)
    total = lax.psum(partial_gram, ("space", "tm"))
    return lax.dynamic_slice_in_dim(total, lax.axis_index("tm") * snaps, snaps, 0)


def solution(mesh):
    placed = (P("space", "tm", None), P(), P(), P())
    return jax.shard_map(
        functools.partial(body, mesh.shape["tm"]),
        mesh=mesh, in_specs=placed, out_specs=P("tm", None), check_vma=False,
    )
```

```python
import functools
import jax
import jax.numpy as jnp
import ml_dtypes
import numpy as np
from jax import lax
from jax.experimental import pallas as pl
from jax.experimental.pallas import tpu as pltpu
from jax.sharding import PartitionSpec as P

STRIDE = 4
STEPS = 4
TILE = 192
SIDE = TILE // STRIDE
ROWS = 2 * STRIDE
CHUNKS = TILE // ROWS
DEPTH = ROWS * TILE
RIM = 4 * TILE
LANES = 128
HALF = 64
F32, BF16 = jnp.float32, jnp.bfloat16
MESH = pl.DeviceIdType.MESH
VMEM_LIMIT = 56 * 1024 * 1024


def coefficient(step_idx):
    return 0.12 + 0.1 * step_idx / max(STEPS - 1, 1)


def stencil_taps():
    taps = np.zeros((2 * STEPS + 1, 2 * STEPS + 1))
    taps[STEPS, STEPS] = 1.0
    for step_idx in range(STEPS):
        padded = np.pad(taps, 1)
        lap = (
            padded[:-2, 1:-1] + padded[2:, 1:-1] + padded[1:-1, :-2] + padded[1:-1, 2:] - 4 * taps
        )
        taps = taps + coefficient(step_idx) * lap
    return taps


TAPS = stencil_taps()
CORNER = 3.0 * float(np.prod([coefficient(k) for k in range(STEPS)]))


def response(row, col, first_row, row_count):
    plane = np.zeros((row_count, TILE))
    for d_row in range(-STEPS, STEPS + 1):
        for d_col in range(-STEPS, STEPS + 1):
            at_row, at_col = row + d_row - first_row, col + d_col
            if 0 <= at_row < row_count and 0 <= at_col < TILE:
                plane[at_row, at_col] = TAPS[d_row + STEPS, d_col + STEPS]
    return plane.reshape(-1)


def split_const(matrix):
    high = matrix.astype(ml_dtypes.bfloat16)
    low = (matrix - high.astype(np.float64)).astype(ml_dtypes.bfloat16)
    return high, low


def along(variant, index):
    return TILE - 2 - STRIDE * index if variant % 2 else 1 + STRIDE * index


def beyond(variant):
    return 3 if variant // 2 else 2


def chunk_matrix():
    matrix = np.zeros((DEPTH, 2 * LANES))

    def put(lane, slot, row, col):
        matrix[:, lane] = response(row, col, 0, ROWS)
        other = row + ROWS if slot == 0 else row - ROWS
        matrix[:, LANES + lane] = response(other, col, 0, ROWS)

    for slot in range(2):
        for index in range(SIDE):
            put(slot * SIDE + index, slot, 1 + STRIDE * slot, 1 + STRIDE * index)
        for side in range(2):
            for variant in range(4):
                col = TILE - 1 + beyond(variant) if side else -beyond(variant)
                row = (2 if variant % 2 else 1) + STRIDE * slot
                put(2 * SIDE + side * 8 + variant * 2 + slot, slot, row, col)
    return matrix


def rim_matrices():
    upper = np.zeros((RIM, 4 * LANES))
    lower = np.zeros((RIM, 4 * LANES))
    for variant in range(4):
        base = variant * LANES
        for index in range(SIDE):
            col = along(variant, index)
            upper[:, base + index] = response(-beyond(variant), col, 0, 4)
            lower[:, base + HALF + index] = response(
                TILE - 1 + beyond(variant), col, TILE - 4, 4
            )
        upper[0, base + SIDE] = 1.0
        upper[TILE - 1, base + SIDE + 1] = 1.0
        lower[3 * TILE, base + HALF + SIDE] = 1.0
        lower[4 * TILE - 1, base + HALF + SIDE + 1] = 1.0
    return upper, lower


def order_matrix():
    matrix = np.zeros((CHUNKS * 16, 4 * LANES))
    for chunk in range(CHUNKS):
        for side in range(2):
            for variant in range(4):
                for slot in range(2):
                    index = 2 * chunk + slot
                    place = SIDE - 1 - index if variant % 2 else index
                    source = chunk * 16 + side * 8 + variant * 2 + slot
                    matrix[source, variant * LANES + side * HALF + place] = 1.0
    return matrix.astype(ml_dtypes.bfloat16)


def place_matrix():
    matrix = np.zeros((CHUNKS, 2 * LANES, LANES))
    for index in range(SIDE):
        chunk, slot = index // 2, index % 2
        matrix[0, index, index] = 1.0
        matrix[CHUNKS - 1, HALF + index, SIDE + index] = 1.0
        matrix[chunk, LANES + index, slot * SIDE] = 1.0
        matrix[chunk, LANES + HALF + index, slot * SIDE + SIDE - 1] = 1.0
    for lane in (SIDE, SIDE + 1, HALF + SIDE, HALF + SIDE + 1):
        matrix[0, lane, 0] = 1.0
    return matrix


def pack(blocks, groups):
    per_group = CHUNKS // groups
    blocks = blocks.reshape((groups, per_group) + blocks.shape[1:])
    spread = blocks[:, per_group - 1]
    kept = []
    for k in range(per_group - 1):
        block = blocks[:, k, ..., : 2 * SIDE]
        rest = spread[..., 32 * k : 32 * (k + 1)] if k < 3 else 0 * spread[..., :32]
        join = np.concatenate if isinstance(blocks, np.ndarray) else jnp.concatenate
        kept.append(join([block, rest], axis=-1))
    stack = np.stack if isinstance(blocks, np.ndarray) else jnp.stack
    return stack(kept, axis=1)


def group_matrices(groups):
    packed = pack(place_matrix(), groups)
    count = packed.shape[1]
    pick = np.zeros((groups, 2 * LANES, LANES))
    place = np.zeros((groups, LANES, count * LANES))
    for group in range(groups):
        flat = packed[group].transpose(1, 0, 2).reshape(2 * LANES, count * LANES)
        needed = np.nonzero(flat.any(axis=1))[0]
        assert len(needed) <= LANES
        for lane, source in enumerate(needed):
            pick[group, source, lane] = 1.0
            place[group, lane] = flat[source]
    return pick.astype(ml_dtypes.bfloat16), place.astype(ml_dtypes.bfloat16)


def split(x):
    high = x.astype(BF16)
    return high, (x - high.astype(F32)).astype(BF16)


def dot(a, b):
    return jnp.dot(a, b, preferred_element_type=F32)


def dot3(a_high, a_low, b_high, b_low):
    return dot(a_high, b_high) + dot(a_low, b_high) + dot(a_high, b_low)


def stencil_kernel(
    tiles, snaps, slots, faces, groups,
    first_ref, ids_ref, table_ref,
    x_ref, area_ref, main_h, main_l, up_h, up_l, down_h, down_l, order_ref,
    out_ref, send_ref,
    high, low, carry, edges, rims,
):
    step = pl.program_id(0)
    first = first_ref[0]
    rows = tiles * snaps
    for t in range(tiles):
        face = lax.rem(ids_ref[first + t], faces)
        part = pl.ds(t * snaps, snaps)
        h, l = split(x_ref[t] * area_ref[pl.ds(face, 1), :])
        high[part, :] = h
        low[part, :] = l
    lane = lax.broadcasted_iota(jnp.int32, (rows, LANES), 1)
    from_before = (lane < SIDE) | ((lane >= 2 * SIDE) & (lane % 2 == 0))
    is_edge = (lane >= 2 * SIDE) & (lane < 2 * SIDE + 16)

    def collect(chunk, value):
        shift = lax.rem(16 * lax.rem(chunk, 8) + LANES - 2 * SIDE, LANES)
        block = lax.div(chunk, 8)
        edges[block] = edges[block] + pltpu.roll(jnp.where(is_edge, value, 0.0), shift, 1)

    @pl.when(step == 0)
    def _():
        carry[...] = jnp.zeros_like(carry)
        edges[...] = jnp.zeros_like(edges)
        rims[...] = dot3(high[:, :RIM], low[:, :RIM], up_h[...], up_l[...])

    result = dot3(high[...], low[...], main_h[...], main_l[...])
    own, other = result[:, :LANES], result[:, LANES:]

    @pl.when(step > 0)
    def _():
        done = out_ref[step - 1] + jnp.where(from_before, 0.0, other)
        out_ref[step - 1] = done
        collect(step - 1, done)

    own = own + jnp.where(from_before, carry[...], 0.0)
    out_ref[step] = own
    carry[...] = other

    @pl.when(step == CHUNKS - 1)
    def _():
        collect(step, own)
        rims[...] = rims[...] + dot3(
            high[:, DEPTH - RIM :], low[:, DEPTH - RIM :], down_h[...], down_l[...]
        )
        sides = jnp.zeros((rows, 4 * LANES), F32)
        for block in range(CHUNKS * 16 // LANES):
            h, l = split(edges[block])
            matrix = order_ref[block * LANES : (block + 1) * LANES, :]
            sides = sides + dot(h, matrix) + dot(l, matrix)
        for group in range(groups):
            base = group * (CHUNKS // groups)
            spread = out_ref[base + CHUNKS // groups - 1]
            for k in range(3):
                piece = pltpu.roll(spread, (2 * SIDE - 32 * k) % LANES, 1)
                out_ref[base + k] = jnp.where(lane < 2 * SIDE, out_ref[base + k], piece)
        low_half = lane[:snaps] < HALF
        for t in range(tiles):
            part = slice(t * snaps, (t + 1) * snaps)
            for pair, source in ((0, rims[part, :]), (1, sides[part, :])):
                chosen = jnp.zeros((snaps, LANES), F32)
                at = (first + t) * 4 + 2 * pair
                kind = [
                    2 * lax.rem(table_ref[slots * 4 + at + k], 2) + table_ref[slots * 8 + at + k]
                    for k in range(2)
                ]
                for variant in range(4):
                    block = source[:, variant * LANES : (variant + 1) * LANES]
                    wanted = jnp.where(
                        low_half,
                        (kind[0] == variant).astype(jnp.int32),
                        (kind[1] == variant).astype(jnp.int32),
                    )
                    chosen = jnp.where(wanted == 1, block, chosen)
                send_ref[t, pair] = chosen


def halo_kernel(
    tiles, snaps, slots, faces, groups,
    first_ref, ids_ref, table_ref,
    strips_ref, root_ref, pick_ref,
    out_ref, weight_ref,
    high, low,
):
    first, me = first_ref[0], first_ref[1]
    lane = lax.broadcasted_iota(jnp.int32, (snaps, LANES), 1)

    def near(slot, edge):
        at = slot * 4 + edge
        return table_ref[at], table_ref[slots * 4 + at], table_ref[slots * 8 + at]

    def corner(slot, edge):
        mid, mid_edge, mid_flip = near(slot, edge)
        other_edge = jnp.where(mid_edge < 2, 2, 0) + mid_flip
        end = lax.rem(mid_edge, 2)
        far, far_edge, far_flip = near(mid, other_edge)
        far_end = jnp.where(far_flip == 1, 1 - end, end)
        side = lax.rem(far_edge, 2)
        row_end = jnp.where(far_edge < 2, side, far_end)
        col_end = jnp.where(far_edge < 2, far_end, side)
        value = strips_ref[far, 0]
        return jnp.where(lane == SIDE + col_end + HALF * row_end, value, 0.0)

    for t in range(tiles):
        slot = first + t
        part = pl.ds(t * snaps, snaps)
        for pair in range(2):
            strips = []
            for k in range(2):
                far, far_edge, _ = near(slot, 2 * pair + k)
                value = strips_ref[far, lax.div(far_edge, 2)]
                rolled = pltpu.roll(value, HALF, 1)
                same = (jnp.zeros((snaps, LANES), jnp.int32) + lax.rem(far_edge, 2)) == k
                strips.append(jnp.where(same, value, rolled))
            both = jnp.where(lane < HALF, strips[0], strips[1])
            both = jnp.where(lane % HALF < SIDE, both, 0.0)
            if pair == 0:
                both = both + CORNER * (corner(slot, 0) + corner(slot, 2))
            h, l = split(both)
            high[part, pair * LANES : (pair + 1) * LANES] = h
            low[part, pair * LANES : (pair + 1) * LANES] = l

    for group in range(groups):
        out_ref[group] = dot(high[...], pick_ref[group]) + dot(low[...], pick_ref[group])
    for t in range(tiles):
        face = lax.rem(ids_ref[first + t], faces)
        for block in range(weight_ref.shape[0]):
            weight_ref[block, t : t + 1, :] = root_ref[me, block, pl.ds(face, 1), :]


def exchange_kernel(groups, src_ref, dst_ref, local_sem, send_sem, recv_sem):
    me = lax.axis_index("tm")
    count = dst_ref.shape[1]
    barrier = pltpu.get_barrier_semaphore()
    for k in range(1, groups):
        pl.semaphore_signal(
            barrier, inc=1, device_id={"tm": lax.rem(me + k, groups)}, device_id_type=MESH
        )
    pl.semaphore_wait(barrier, groups - 1)
    copies = []
    for k in sorted(range(1, groups), key=lambda k: abs(k - groups // 2)):
        to = lax.rem(me + k, groups)
        copy = pltpu.make_async_remote_copy(
            src_ref=src_ref.at[to, pl.ds(0, count)],
            dst_ref=dst_ref.at[me],
            send_sem=send_sem.at[k],
            recv_sem=recv_sem.at[k],
            device_id={"tm": to},
            device_id_type=MESH,
        )
        copy.start()
        copies.append(copy)
    own = pltpu.make_async_copy(src_ref.at[me, pl.ds(0, count)], dst_ref.at[me], local_sem)
    own.start()
    own.wait()
    for copy in copies:
        copy.wait()


def gram_kernel(
    tiles, snaps, groups, spaces, scale,
    shared_ref, halo_ref, weight_ref, place_ref,
    out_ref,
    strips, high, low, part, from_tm, from_space,
    strip_sems, tm_sems, space_sems,
):
    me = lax.axis_index("tm")
    here = lax.axis_index("space")
    barrier = pltpu.get_barrier_semaphore()
    for k in range(1, groups):
        pl.semaphore_signal(
            barrier, inc=1, device_id={"tm": lax.rem(me + k, groups)}, device_id_type=MESH
        )
    for k in range(1, spaces):
        pl.semaphore_signal(
            barrier, inc=1, device_id={"space": lax.rem(here + k, spaces)}, device_id_type=MESH
        )
    pl.semaphore_wait(barrier, groups + spaces - 2)

    def send(src, dst, sems, k, device):
        copy = pltpu.make_async_remote_copy(
            src_ref=src,
            dst_ref=dst,
            send_sem=sems.at[0, k],
            recv_sem=sems.at[1, k],
            device_id=device,
            device_id_type=MESH,
        )
        copy.start()
        return copy

    copies = []
    for k in range(1, groups):
        to = lax.rem(me + k, groups)
        copies.append(send(halo_ref.at[to], strips.at[k], strip_sems, k, {"tm": to}))
    strips[0] = halo_ref[me]
    for copy in copies:
        copy.wait()

    blocks = shared_ref.shape[1]
    place = place_ref[me]
    for group in range(groups):
        h, l = split(strips[lax.rem(me - group + groups, groups)])
        rows = slice(group * snaps, (group + 1) * snaps)
        for block in range(blocks):
            matrix = place[:, block * LANES : (block + 1) * LANES]
            added = dot(h, matrix) + dot(l, matrix) + shared_ref[group, block]
            for t in range(tiles):
                x = added[t * snaps : (t + 1) * snaps] * weight_ref[block, t : t + 1, :]
                xh, xl = split(x)
                at = (block * tiles + t) * LANES
                high[rows, at : at + LANES] = xh
                low[rows, at : at + LANES] = xl
    dims = (((1,), (1,)), ((), ()))
    main = lax.dot_general(high[...], high[...], dims, preferred_element_type=F32)
    cross = lax.dot_general(high[...], low[...], dims, preferred_element_type=F32)
    part[...] = ((main + cross + cross.T) * scale).reshape(part.shape)

    copies = []
    for k in range(1, groups):
        to = lax.rem(me + k, groups)
        copies.append(send(part.at[to], from_tm.at[k], tm_sems, k, {"tm": to}))
    for copy in copies:
        copy.wait()
    total = part[me]
    for k in range(1, groups):
        total = total + from_tm[k]
    from_space[0] = total
    copies = []
    for k in range(1, spaces):
        to = lax.rem(here + k, spaces)
        copies.append(send(from_space.at[0], from_space.at[k], space_sems, k, {"space": to}))
    for copy in copies:
        copy.wait()
    total = from_space[here]
    for source in range(1, spaces):
        total = total + from_space[lax.rem(here - source + spaces, spaces)]
    out_ref[...] = total


def full(shape):
    return pl.BlockSpec(shape, lambda c, *_: (0,) * len(shape))


def body(groups, spaces, pw_field, cell_area, tile_ids, edge_table):
    tiles, snaps, cells = pw_field.shape
    slots, faces = tile_ids.shape[0], cell_area.shape[0]
    rows = tiles * snaps
    first = jnp.stack([lax.axis_index("space") * tiles, lax.axis_index("tm")]).astype(jnp.int32)
    table = edge_table.reshape(-1)
    main_h, main_l = split_const(chunk_matrix())
    upper, lower = rim_matrices()
    up_h, up_l = split_const(upper)
    down_h, down_l = split_const(lower)

    sums, send = pl.pallas_call(
        functools.partial(stencil_kernel, tiles, snaps, slots, faces, groups),
        grid_spec=pltpu.PrefetchScalarGridSpec(
            num_scalar_prefetch=3,
            grid=(CHUNKS,),
            in_specs=[
                pl.BlockSpec((tiles, snaps, DEPTH), lambda c, *_: (0, 0, c)),
                pl.BlockSpec((faces, DEPTH), lambda c, *_: (0, c)),
                full((DEPTH, 2 * LANES)),
                full((DEPTH, 2 * LANES)),
                full((RIM, 4 * LANES)),
                full((RIM, 4 * LANES)),
                full((RIM, 4 * LANES)),
                full((RIM, 4 * LANES)),
                full((CHUNKS * 16, 4 * LANES)),
            ],
            out_specs=[full((CHUNKS, rows, LANES)), full((tiles, 2, snaps, LANES))],
            scratch_shapes=[
                pltpu.VMEM((rows, DEPTH), BF16),
                pltpu.VMEM((rows, DEPTH), BF16),
                pltpu.VMEM((rows, LANES), F32),
                pltpu.VMEM((CHUNKS * 16 // LANES, rows, LANES), F32),
                pltpu.VMEM((rows, 4 * LANES), F32),
            ],
        ),
        out_shape=[
            jax.ShapeDtypeStruct((CHUNKS, rows, LANES), F32),
            jax.ShapeDtypeStruct((tiles, 2, snaps, LANES), F32),
        ],
        compiler_params=pltpu.CompilerParams(vmem_limit_bytes=VMEM_LIMIT),
        name="stencil",
    )(
        first, tile_ids, table, pw_field, cell_area,
        main_h, main_l, up_h, up_l, down_h, down_l, order_matrix(),
    )

    strips = lax.all_gather(send, "space", axis=0, tiled=True)

    sampled = cell_area.reshape(faces, TILE, TILE)[:, 1::STRIDE, 1::STRIDE]
    root = jnp.sqrt(1.0 / sampled).reshape(faces, CHUNKS, 2 * SIDE)
    root = jnp.pad(root, ((0, 0), (0, 0), (0, LANES - 2 * SIDE)))
    root = pack(jnp.transpose(root, (1, 0, 2)), groups)
    pick, place = group_matrices(groups)
    blocks = root.shape[1]

    shared = pl.pallas_call(
        functools.partial(exchange_kernel, groups),
        in_specs=[pl.BlockSpec(memory_space=pl.ANY)],
        out_specs=pl.BlockSpec(memory_space=pl.ANY),
        scratch_shapes=[
            pltpu.SemaphoreType.DMA,
            pltpu.SemaphoreType.DMA((groups,)),
            pltpu.SemaphoreType.DMA((groups,)),
        ],
        out_shape=jax.ShapeDtypeStruct((groups, blocks, rows, LANES), F32),
        compiler_params=pltpu.CompilerParams(
            collective_id=0, has_side_effects=True, vmem_limit_bytes=VMEM_LIMIT
        ),
        cost_estimate=pl.CostEstimate(
            flops=0, bytes_accessed=32 * CHUNKS * rows * LANES, transcendentals=0
        ),
        name="exchange",
    )(sums.reshape(groups, CHUNKS // groups, rows, LANES))

    halos, weights = pl.pallas_call(
        functools.partial(halo_kernel, tiles, snaps, slots, faces, groups),
        grid_spec=pltpu.PrefetchScalarGridSpec(
            num_scalar_prefetch=3,
            grid=(1,),
            in_specs=[
                full((slots, 2, snaps, LANES)),
                full((groups, blocks, faces, LANES)),
                full((groups, 2 * LANES, LANES)),
            ],
            out_specs=[full((groups, rows, LANES)), full((blocks, tiles, LANES))],
            scratch_shapes=[
                pltpu.VMEM((rows, 2 * LANES), BF16),
                pltpu.VMEM((rows, 2 * LANES), BF16),
            ],
        ),
        out_shape=[
            jax.ShapeDtypeStruct((groups, rows, LANES), F32),
            jax.ShapeDtypeStruct((blocks, tiles, LANES), F32),
        ],
        compiler_params=pltpu.CompilerParams(vmem_limit_bytes=VMEM_LIMIT),
        name="halo",
    )(first, tile_ids, table, strips, root, pick)

    count = groups * snaps
    return pl.pallas_call(
        functools.partial(gram_kernel, tiles, snaps, groups, spaces, 1.0 / (slots * SIDE * SIDE)),
        in_specs=[pl.BlockSpec(memory_space=pltpu.VMEM)] * 4,
        out_specs=pl.BlockSpec(memory_space=pltpu.VMEM),
        scratch_shapes=[
            pltpu.VMEM((groups, rows, LANES), F32),
            pltpu.VMEM((count, tiles * blocks * LANES), BF16),
            pltpu.VMEM((count, tiles * blocks * LANES), BF16),
            pltpu.VMEM((groups, snaps, count), F32),
            pltpu.VMEM((groups, snaps, count), F32),
            pltpu.VMEM((spaces, snaps, count), F32),
            pltpu.SemaphoreType.DMA((2, groups)),
            pltpu.SemaphoreType.DMA((2, groups)),
            pltpu.SemaphoreType.DMA((2, spaces)),
        ],
        out_shape=jax.ShapeDtypeStruct((snaps, count), F32),
        compiler_params=pltpu.CompilerParams(
            collective_id=1, has_side_effects=True, vmem_limit_bytes=VMEM_LIMIT
        ),
        name="gram",
    )(shared, halos, weights, place)


def solution(mesh):
    placed = (P("space", "tm", None), P(), P(), P())
    return jax.shard_map(
        functools.partial(body, mesh.shape["tm"], mesh.shape["space"]),
        mesh=mesh, in_specs=placed, out_specs=P("tm", None), check_vma=False,
    )
```

```python
import functools
import jax
import jax.numpy as jnp
import ml_dtypes
import numpy as np
from jax import lax
from jax.experimental import pallas as pl
from jax.experimental.pallas import tpu as pltpu
from jax.sharding import PartitionSpec as P

STRIDE = 4
STEPS = 4
TILE = 192
SIDE = TILE // STRIDE
ROWS = 2 * STRIDE
CHUNKS = TILE // ROWS
DEPTH = ROWS * TILE
RIM = 4 * TILE
LANES = 128
HALF = 64
F32, BF16 = jnp.float32, jnp.bfloat16
MESH = pl.DeviceIdType.MESH
VMEM_LIMIT = 56 * 1024 * 1024


def coefficient(step_idx):
    return 0.12 + 0.1 * step_idx / max(STEPS - 1, 1)


def stencil_taps():
    taps = np.zeros((2 * STEPS + 1, 2 * STEPS + 1))
    taps[STEPS, STEPS] = 1.0
    for step_idx in range(STEPS):
        padded = np.pad(taps, 1)
        lap = (
            padded[:-2, 1:-1] + padded[2:, 1:-1] + padded[1:-1, :-2] + padded[1:-1, 2:] - 4 * taps
        )
        taps = taps + coefficient(step_idx) * lap
    return taps


TAPS = stencil_taps()
CORNER = 3.0 * float(np.prod([coefficient(k) for k in range(STEPS)]))


def response(row, col, first_row, row_count):
    plane = np.zeros((row_count, TILE))
    for d_row in range(-STEPS, STEPS + 1):
        for d_col in range(-STEPS, STEPS + 1):
            at_row, at_col = row + d_row - first_row, col + d_col
            if 0 <= at_row < row_count and 0 <= at_col < TILE:
                plane[at_row, at_col] = TAPS[d_row + STEPS, d_col + STEPS]
    return plane.reshape(-1)


def split_const(matrix):
    high = matrix.astype(ml_dtypes.bfloat16)
    low = (matrix - high.astype(np.float64)).astype(ml_dtypes.bfloat16)
    return high, low


def along(variant, index):
    return TILE - 2 - STRIDE * index if variant % 2 else 1 + STRIDE * index


def beyond(variant):
    return 3 if variant // 2 else 2


def chunk_matrix():
    matrix = np.zeros((DEPTH, 2 * LANES))

    def put(lane, slot, row, col):
        matrix[:, lane] = response(row, col, 0, ROWS)
        other = row + ROWS if slot == 0 else row - ROWS
        matrix[:, LANES + lane] = response(other, col, 0, ROWS)

    for slot in range(2):
        for index in range(SIDE):
            put(slot * SIDE + index, slot, 1 + STRIDE * slot, 1 + STRIDE * index)
        for side in range(2):
            for variant in range(4):
                col = TILE - 1 + beyond(variant) if side else -beyond(variant)
                row = (2 if variant % 2 else 1) + STRIDE * slot
                put(2 * SIDE + side * 8 + variant * 2 + slot, slot, row, col)
    return matrix


def rim_matrices():
    upper = np.zeros((RIM, 4 * LANES))
    lower = np.zeros((RIM, 4 * LANES))
    for variant in range(4):
        base = variant * LANES
        for index in range(SIDE):
            col = along(variant, index)
            upper[:, base + index] = response(-beyond(variant), col, 0, 4)
            lower[:, base + HALF + index] = response(
                TILE - 1 + beyond(variant), col, TILE - 4, 4
            )
        upper[0, base + SIDE] = 1.0
        upper[TILE - 1, base + SIDE + 1] = 1.0
        lower[3 * TILE, base + HALF + SIDE] = 1.0
        lower[4 * TILE - 1, base + HALF + SIDE + 1] = 1.0
    return upper, lower


def order_matrix():
    matrix = np.zeros((CHUNKS * 16, 4 * LANES))
    for chunk in range(CHUNKS):
        for side in range(2):
            for variant in range(4):
                for slot in range(2):
                    index = 2 * chunk + slot
                    place = SIDE - 1 - index if variant % 2 else index
                    source = chunk * 16 + side * 8 + variant * 2 + slot
                    matrix[source, variant * LANES + side * HALF + place] = 1.0
    return matrix.astype(ml_dtypes.bfloat16)


def place_matrix():
    matrix = np.zeros((CHUNKS, 2 * LANES, LANES))
    for index in range(SIDE):
        chunk, slot = index // 2, index % 2
        matrix[0, index, index] = 1.0
        matrix[CHUNKS - 1, HALF + index, SIDE + index] = 1.0
        matrix[chunk, LANES + index, slot * SIDE] = 1.0
        matrix[chunk, LANES + HALF + index, slot * SIDE + SIDE - 1] = 1.0
    for lane in (SIDE, SIDE + 1, HALF + SIDE, HALF + SIDE + 1):
        matrix[0, lane, 0] = 1.0
    return matrix


def pack(blocks, groups):
    per_group = CHUNKS // groups
    blocks = blocks.reshape((groups, per_group) + blocks.shape[1:])
    spread = blocks[:, per_group - 1]
    kept = []
    for k in range(per_group - 1):
        block = blocks[:, k, ..., : 2 * SIDE]
        rest = spread[..., 32 * k : 32 * (k + 1)] if k < 3 else 0 * spread[..., :32]
        join = np.concatenate if isinstance(blocks, np.ndarray) else jnp.concatenate
        kept.append(join([block, rest], axis=-1))
    stack = np.stack if isinstance(blocks, np.ndarray) else jnp.stack
    return stack(kept, axis=1)


def group_matrices(groups):
    packed = pack(place_matrix(), groups)
    count = packed.shape[1]
    pick = np.zeros((groups, 2 * LANES, LANES))
    place = np.zeros((groups, LANES, count * LANES))
    for group in range(groups):
        flat = packed[group].transpose(1, 0, 2).reshape(2 * LANES, count * LANES)
        needed = np.nonzero(flat.any(axis=1))[0]
        assert len(needed) <= LANES
        for lane, source in enumerate(needed):
            pick[group, source, lane] = 1.0
            place[group, lane] = flat[source]
    return pick.astype(ml_dtypes.bfloat16), place.astype(ml_dtypes.bfloat16)


def split(x):
    high = x.astype(BF16)
    return high, (x - high.astype(F32)).astype(BF16)


def dot(a, b):
    return jnp.dot(a, b, preferred_element_type=F32)


def dot3(a_high, a_low, b_high, b_low):
    return dot(a_high, b_high) + dot(a_low, b_high) + dot(a_high, b_low)


def stencil_kernel(
    tiles, snaps, slots, faces, groups,
    first_ref, ids_ref, table_ref,
    x_ref, area_ref, main_h, main_l, up_h, up_l, down_h, down_l, order_ref,
    out_ref, send_ref,
    high, low, carry, edges, rims,
):
    step = pl.program_id(0)
    first = first_ref[0]
    rows = tiles * snaps
    result = jnp.zeros((rows, 2 * LANES), F32)
    for half in range(2):
        cells = slice(half * RIM, (half + 1) * RIM)
        for t in range(tiles):
            face = lax.rem(ids_ref[first + t], faces)
            part = slice(t * snaps, (t + 1) * snaps)
            h, l = split(x_ref[t, :, cells] * area_ref[pl.ds(face, 1), cells])
            high[part, cells] = h
            low[part, cells] = l
        result = result + dot3(high[:, cells], low[:, cells], main_h[cells, :], main_l[cells, :])
    lane = lax.broadcasted_iota(jnp.int32, (rows, LANES), 1)
    from_before = (lane < SIDE) | ((lane >= 2 * SIDE) & (lane % 2 == 0))
    is_edge = (lane >= 2 * SIDE) & (lane < 2 * SIDE + 16)

    def collect(chunk, value):
        shift = lax.rem(16 * lax.rem(chunk, 8) + LANES - 2 * SIDE, LANES)
        block = lax.div(chunk, 8)
        edges[block] = edges[block] + pltpu.roll(jnp.where(is_edge, value, 0.0), shift, 1)

    @pl.when(step == 0)
    def _():
        carry[...] = jnp.zeros_like(carry)
        edges[...] = jnp.zeros_like(edges)
        rims[...] = dot3(high[:, :RIM], low[:, :RIM], up_h[...], up_l[...])

    own, other = result[:, :LANES], result[:, LANES:]

    @pl.when(step > 0)
    def _():
        done = out_ref[step - 1] + jnp.where(from_before, 0.0, other)
        out_ref[step - 1] = done
        collect(step - 1, done)

    own = own + jnp.where(from_before, carry[...], 0.0)
    out_ref[step] = own
    carry[...] = other

    @pl.when(step == CHUNKS - 1)
    def _():
        collect(step, own)
        rims[...] = rims[...] + dot3(
            high[:, DEPTH - RIM :], low[:, DEPTH - RIM :], down_h[...], down_l[...]
        )
        sides = jnp.zeros((rows, 4 * LANES), F32)
        for block in range(CHUNKS * 16 // LANES):
            h, l = split(edges[block])
            matrix = order_ref[block * LANES : (block + 1) * LANES, :]
            sides = sides + dot(h, matrix) + dot(l, matrix)
        for group in range(groups):
            base = group * (CHUNKS // groups)
            spread = out_ref[base + CHUNKS // groups - 1]
            for k in range(3):
                piece = pltpu.roll(spread, (2 * SIDE - 32 * k) % LANES, 1)
                out_ref[base + k] = jnp.where(lane < 2 * SIDE, out_ref[base + k], piece)
        low_half = lane[:snaps] < HALF
        for t in range(tiles):
            part = slice(t * snaps, (t + 1) * snaps)
            for pair, source in ((0, rims[part, :]), (1, sides[part, :])):
                chosen = jnp.zeros((snaps, LANES), F32)
                at = (first + t) * 4 + 2 * pair
                kind = [
                    2 * lax.rem(table_ref[slots * 4 + at + k], 2) + table_ref[slots * 8 + at + k]
                    for k in range(2)
                ]
                for variant in range(4):
                    block = source[:, variant * LANES : (variant + 1) * LANES]
                    wanted = jnp.where(
                        low_half,
                        (kind[0] == variant).astype(jnp.int32),
                        (kind[1] == variant).astype(jnp.int32),
                    )
                    chosen = jnp.where(wanted == 1, block, chosen)
                send_ref[t, pair] = chosen


def halo_kernel(
    tiles, snaps, slots, faces, groups,
    first_ref, ids_ref, table_ref,
    strips_ref, root_ref, pick_ref,
    out_ref, weight_ref,
    high, low,
):
    first, me = first_ref[0], first_ref[1]
    lane = lax.broadcasted_iota(jnp.int32, (snaps, LANES), 1)

    def near(slot, edge):
        at = slot * 4 + edge
        return table_ref[at], table_ref[slots * 4 + at], table_ref[slots * 8 + at]

    def corner(slot, edge):
        mid, mid_edge, mid_flip = near(slot, edge)
        other_edge = jnp.where(mid_edge < 2, 2, 0) + mid_flip
        end = lax.rem(mid_edge, 2)
        far, far_edge, far_flip = near(mid, other_edge)
        far_end = jnp.where(far_flip == 1, 1 - end, end)
        side = lax.rem(far_edge, 2)
        row_end = jnp.where(far_edge < 2, side, far_end)
        col_end = jnp.where(far_edge < 2, far_end, side)
        value = strips_ref[far, 0]
        return jnp.where(lane == SIDE + col_end + HALF * row_end, value, 0.0)

    for t in range(tiles):
        slot = first + t
        part = pl.ds(t * snaps, snaps)
        for pair in range(2):
            strips = []
            for k in range(2):
                far, far_edge, _ = near(slot, 2 * pair + k)
                value = strips_ref[far, lax.div(far_edge, 2)]
                rolled = pltpu.roll(value, HALF, 1)
                same = (jnp.zeros((snaps, LANES), jnp.int32) + lax.rem(far_edge, 2)) == k
                strips.append(jnp.where(same, value, rolled))
            both = jnp.where(lane < HALF, strips[0], strips[1])
            both = jnp.where(lane % HALF < SIDE, both, 0.0)
            if pair == 0:
                both = both + CORNER * (corner(slot, 0) + corner(slot, 2))
            h, l = split(both)
            high[part, pair * LANES : (pair + 1) * LANES] = h
            low[part, pair * LANES : (pair + 1) * LANES] = l

    for group in range(groups):
        out_ref[group] = dot(high[...], pick_ref[group]) + dot(low[...], pick_ref[group])
    for t in range(tiles):
        face = lax.rem(ids_ref[first + t], faces)
        for block in range(weight_ref.shape[0]):
            weight_ref[block, t : t + 1, :] = root_ref[me, block, pl.ds(face, 1), :]


def exchange_kernel(groups, src_ref, dst_ref, local_sem, send_sem, recv_sem):
    me = lax.axis_index("tm")
    count = dst_ref.shape[1]
    barrier = pltpu.get_barrier_semaphore()
    for k in range(1, groups):
        pl.semaphore_signal(
            barrier, inc=1, device_id={"tm": lax.rem(me + k, groups)}, device_id_type=MESH
        )
    pl.semaphore_wait(barrier, groups - 1)
    copies = []
    for k in sorted(range(1, groups), key=lambda k: abs(k - groups // 2)):
        to = lax.rem(me + k, groups)
        copy = pltpu.make_async_remote_copy(
            src_ref=src_ref.at[to, pl.ds(0, count)],
            dst_ref=dst_ref.at[me],
            send_sem=send_sem.at[k],
            recv_sem=recv_sem.at[k],
            device_id={"tm": to},
            device_id_type=MESH,
        )
        copy.start()
        copies.append(copy)
    own = pltpu.make_async_copy(src_ref.at[me, pl.ds(0, count)], dst_ref.at[me], local_sem)
    own.start()
    own.wait()
    for copy in copies:
        copy.wait()


def gram_kernel(
    tiles, snaps, groups, spaces, scale,
    shared_ref, halo_ref, weight_ref, place_ref,
    out_ref,
    strips, high, low, part, from_tm, from_space,
    strip_sems, tm_sems, space_sems,
):
    me = lax.axis_index("tm")
    here = lax.axis_index("space")
    barrier = pltpu.get_barrier_semaphore()
    for k in range(1, groups):
        pl.semaphore_signal(
            barrier, inc=1, device_id={"tm": lax.rem(me + k, groups)}, device_id_type=MESH
        )
    for k in range(1, spaces):
        pl.semaphore_signal(
            barrier, inc=1, device_id={"space": lax.rem(here + k, spaces)}, device_id_type=MESH
        )
    pl.semaphore_wait(barrier, groups + spaces - 2)

    def send(src, dst, sems, k, device):
        copy = pltpu.make_async_remote_copy(
            src_ref=src,
            dst_ref=dst,
            send_sem=sems.at[0, k],
            recv_sem=sems.at[1, k],
            device_id=device,
            device_id_type=MESH,
        )
        copy.start()
        return copy

    copies = []
    for k in range(1, groups):
        to = lax.rem(me + k, groups)
        copies.append(send(halo_ref.at[to], strips.at[k], strip_sems, k, {"tm": to}))
    strips[0] = halo_ref[me]
    for copy in copies:
        copy.wait()

    blocks = shared_ref.shape[1]
    place = place_ref[me]
    for group in range(groups):
        h, l = split(strips[lax.rem(me - group + groups, groups)])
        rows = slice(group * snaps, (group + 1) * snaps)
        for block in range(blocks):
            matrix = place[:, block * LANES : (block + 1) * LANES]
            added = dot(h, matrix) + dot(l, matrix) + shared_ref[group, block]
            for t in range(tiles):
                x = added[t * snaps : (t + 1) * snaps] * weight_ref[block, t : t + 1, :]
                xh, xl = split(x)
                at = (block * tiles + t) * LANES
                high[rows, at : at + LANES] = xh
                low[rows, at : at + LANES] = xl
    dims = (((1,), (1,)), ((), ()))
    main = lax.dot_general(high[...], high[...], dims, preferred_element_type=F32)
    cross = lax.dot_general(high[...], low[...], dims, preferred_element_type=F32)
    part[...] = ((main + cross + cross.T) * scale).reshape(part.shape)

    copies = []
    for k in range(1, groups):
        to = lax.rem(me + k, groups)
        copies.append(send(part.at[to], from_tm.at[k], tm_sems, k, {"tm": to}))
    for copy in copies:
        copy.wait()
    total = part[me]
    for k in range(1, groups):
        total = total + from_tm[k]
    from_space[0] = total
    copies = []
    for k in range(1, spaces):
        to = lax.rem(here + k, spaces)
        copies.append(send(from_space.at[0], from_space.at[k], space_sems, k, {"space": to}))
    for copy in copies:
        copy.wait()
    total = from_space[here]
    for source in range(1, spaces):
        total = total + from_space[lax.rem(here - source + spaces, spaces)]
    out_ref[...] = total


def full(shape):
    return pl.BlockSpec(shape, lambda c, *_: (0,) * len(shape))


def body(groups, spaces, pw_field, cell_area, tile_ids, edge_table):
    tiles, snaps, cells = pw_field.shape
    slots, faces = tile_ids.shape[0], cell_area.shape[0]
    rows = tiles * snaps
    first = jnp.stack([lax.axis_index("space") * tiles, lax.axis_index("tm")]).astype(jnp.int32)
    table = edge_table.reshape(-1)
    main_h, main_l = split_const(chunk_matrix())
    upper, lower = rim_matrices()
    up_h, up_l = split_const(upper)
    down_h, down_l = split_const(lower)

    sums, send = pl.pallas_call(
        functools.partial(stencil_kernel, tiles, snaps, slots, faces, groups),
        grid_spec=pltpu.PrefetchScalarGridSpec(
            num_scalar_prefetch=3,
            grid=(CHUNKS,),
            in_specs=[
                pl.BlockSpec((tiles, snaps, DEPTH), lambda c, *_: (0, 0, c)),
                pl.BlockSpec((faces, DEPTH), lambda c, *_: (0, c)),
                full((DEPTH, 2 * LANES)),
                full((DEPTH, 2 * LANES)),
                full((RIM, 4 * LANES)),
                full((RIM, 4 * LANES)),
                full((RIM, 4 * LANES)),
                full((RIM, 4 * LANES)),
                full((CHUNKS * 16, 4 * LANES)),
            ],
            out_specs=[full((CHUNKS, rows, LANES)), full((tiles, 2, snaps, LANES))],
            scratch_shapes=[
                pltpu.VMEM((rows, DEPTH), BF16),
                pltpu.VMEM((rows, DEPTH), BF16),
                pltpu.VMEM((rows, LANES), F32),
                pltpu.VMEM((CHUNKS * 16 // LANES, rows, LANES), F32),
                pltpu.VMEM((rows, 4 * LANES), F32),
            ],
        ),
        out_shape=[
            jax.ShapeDtypeStruct((CHUNKS, rows, LANES), F32),
            jax.ShapeDtypeStruct((tiles, 2, snaps, LANES), F32),
        ],
        compiler_params=pltpu.CompilerParams(vmem_limit_bytes=VMEM_LIMIT),
        name="stencil",
    )(
        first, tile_ids, table, pw_field, cell_area,
        main_h, main_l, up_h, up_l, down_h, down_l, order_matrix(),
    )

    strips = lax.all_gather(send, "space", axis=0, tiled=True)

    sampled = cell_area.reshape(faces, TILE, TILE)[:, 1::STRIDE, 1::STRIDE]
    root = jnp.sqrt(1.0 / sampled).reshape(faces, CHUNKS, 2 * SIDE)
    root = jnp.pad(root, ((0, 0), (0, 0), (0, LANES - 2 * SIDE)))
    root = pack(jnp.transpose(root, (1, 0, 2)), groups)
    pick, place = group_matrices(groups)
    blocks = root.shape[1]

    shared = pl.pallas_call(
        functools.partial(exchange_kernel, groups),
        in_specs=[pl.BlockSpec(memory_space=pl.ANY)],
        out_specs=pl.BlockSpec(memory_space=pl.ANY),
        scratch_shapes=[
            pltpu.SemaphoreType.DMA,
            pltpu.SemaphoreType.DMA((groups,)),
            pltpu.SemaphoreType.DMA((groups,)),
        ],
        out_shape=jax.ShapeDtypeStruct((groups, blocks, rows, LANES), F32),
        compiler_params=pltpu.CompilerParams(
            collective_id=0, has_side_effects=True, vmem_limit_bytes=VMEM_LIMIT
        ),
        cost_estimate=pl.CostEstimate(
            flops=0, bytes_accessed=32 * CHUNKS * rows * LANES, transcendentals=0
        ),
        name="exchange",
    )(sums.reshape(groups, CHUNKS // groups, rows, LANES))

    halos, weights = pl.pallas_call(
        functools.partial(halo_kernel, tiles, snaps, slots, faces, groups),
        grid_spec=pltpu.PrefetchScalarGridSpec(
            num_scalar_prefetch=3,
            grid=(1,),
            in_specs=[
                full((slots, 2, snaps, LANES)),
                full((groups, blocks, faces, LANES)),
                full((groups, 2 * LANES, LANES)),
            ],
            out_specs=[full((groups, rows, LANES)), full((blocks, tiles, LANES))],
            scratch_shapes=[
                pltpu.VMEM((rows, 2 * LANES), BF16),
                pltpu.VMEM((rows, 2 * LANES), BF16),
            ],
        ),
        out_shape=[
            jax.ShapeDtypeStruct((groups, rows, LANES), F32),
            jax.ShapeDtypeStruct((blocks, tiles, LANES), F32),
        ],
        compiler_params=pltpu.CompilerParams(vmem_limit_bytes=VMEM_LIMIT),
        name="halo",
    )(first, tile_ids, table, strips, root, pick)

    count = groups * snaps
    return pl.pallas_call(
        functools.partial(gram_kernel, tiles, snaps, groups, spaces, 1.0 / (slots * SIDE * SIDE)),
        in_specs=[pl.BlockSpec(memory_space=pltpu.VMEM)] * 4,
        out_specs=pl.BlockSpec(memory_space=pltpu.VMEM),
        scratch_shapes=[
            pltpu.VMEM((groups, rows, LANES), F32),
            pltpu.VMEM((count, tiles * blocks * LANES), BF16),
            pltpu.VMEM((count, tiles * blocks * LANES), BF16),
            pltpu.VMEM((groups, snaps, count), F32),
            pltpu.VMEM((groups, snaps, count), F32),
            pltpu.VMEM((spaces, snaps, count), F32),
            pltpu.SemaphoreType.DMA((2, groups)),
            pltpu.SemaphoreType.DMA((2, groups)),
            pltpu.SemaphoreType.DMA((2, spaces)),
        ],
        out_shape=jax.ShapeDtypeStruct((snaps, count), F32),
        compiler_params=pltpu.CompilerParams(
            collective_id=1, has_side_effects=True, vmem_limit_bytes=VMEM_LIMIT
        ),
        name="gram",
    )(shared, halos, weights, place)


def solution(mesh):
    placed = (P("space", "tm", None), P(), P(), P())
    return jax.shard_map(
        functools.partial(body, mesh.shape["tm"], mesh.shape["space"]),
        mesh=mesh, in_specs=placed, out_specs=P("tm", None), check_vma=False,
    )
```
